32 devices in a mesh: parts: 2 (over y), replica: 8 (over z, core), tensor: 2 (over x).
Axes of the slice: x: 2, y: 2, z: 4, core: 2. Of those that a mesh axis runs over, the one named last changes fastest.
Arguments:
- queries: bfloat16 [4, 2048, 4096], P(None, ('parts', 'replica'), 'tensor'), parts along dimension 1, may hold values from -9 to 9
- step_keys: bfloat16 [4, 2048, 1024], P(None, ('parts', 'replica'), 'tensor'), parts along dimension 1, may hold values from -4 to 4
- step_values: bfloat16 [4, 2048, 1024], P(None, ('parts', 'replica'), 'tensor'), parts along dimension 1, may hold values from -4 to 4
- cached_key_rows: bfloat16 [2048, 8, 32, 128], P(('parts', 'replica'), 'tensor'), parts along dimension 0, may hold values from -4 to 4
- cached_value_rows: bfloat16 [2048, 8, 32, 128], P(('parts', 'replica'), 'tensor'), parts along dimension 0, may hold values from -4 to 4
- cache_length: int32 [2048], P(('parts', 'replica')), parts along dimension 0, may hold values from 2 to 32
- output_weight: bfloat16 [4096, 8192], P(None, 'tensor'), may hold values from -0.09375 to 0.09375
- adapter_down_bank: bfloat16 [256, 16, 4096], P(('parts', 'replica'), None, 'tensor'), parts along dimension 0, may hold values from -0.09375 to 0.09375
- adapter_up_bank: bfloat16 [256, 16, 8192], P(('parts', 'replica'), None, 'tensor'), parts along dimension 0, may hold values from -1.5 to 1.5
- adapter_bank_row: int32 [256], P('parts'), parts along dimension 0, may hold values from 0 to 127, as said below
- segment_adapter: int32 [16, 64], P(('parts', 'replica')), parts along dimension 0, may hold values from 0 to 127, as said below
- request_segment_index: int32 [16, 128], P(('parts', 'replica')), parts along dimension 0, may hold values from 0 to 63, never falling along the last dimension, each value on 1 to 6 neighbouring positions
Outputs:
- projected: bfloat16 [4, 2048, 8192], P(None, ('parts', 'replica'), 'tensor'), parts along dimension 1
The draws below stay inside these ranges and needn't reach their ends.
There are 2 independent parts, one for each index of `parts`. The reference program is written for one: setup_inputs(seed, part) draws one part's arguments, and reference() takes and returns one part's arrays. A program takes and returns all parts, laid end to end along the dimension named above; an argument that names none is the same for every part. Nothing has to cross between parts.
Inputs may be any that keep to these rules, and one draw needn't show every extreme that they name: `adapter_bank_row`: a permutation of the 128 bank rows. `segment_adapter`: each row lists 64 distinct adapters; in each row at most 16 of them have adapter_bank_row values in one aligned block of 16 bank rows, and some block of every row holds exactly 16. `request_segment_index`: each row's segment numbers never fall; every segment number of 0 to 63 holds 1 to 6 requests, one exactly 6.
All inputs are finite; a program needn't handle non-finite values.
Results may differ from the reference program's by a relative error of at most 0.0062.
Values may be sent and summed in bfloat16 or wider, within the bound.
A program may use at most 192 MiB of HBM per device.

```python
import math
import jax
import jax.numpy as jnp
import numpy as np
from jax import lax

MODEL_WIDTH = 8192
QUERY_HEADS = 32
KV = 8
HEAD_SIZE = 128
ADAPTER_RANK = 16
STEPS = 4
SEG_MOST = 6
BATCH_DEV = 128
ADAPT_DEV = 16
CACHE = 32
BATCH = 1024
ADAPTER_TOTAL = 128
SEGS = 64
MOST = 16
N_REPLICA = 8


def bank_order(key):
    sub_key = jax.random.fold_in(key, 101)
    scores = jax.random.randint(sub_key, (ADAPTER_TOTAL,), 0, 1 << 16) * ADAPTER_TOTAL + jnp.arange(ADAPTER_TOTAL)
    return jnp.argsort(scores).astype(jnp.int32)


def draw_adapter_bank_row(key, part):
    order = bank_order(key)
    return order


def draw_segment_adapter(key, part):
    order = bank_order(key)
    inverse = jnp.argsort(order).astype(jnp.int32)
    key = jax.random.fold_in(key, 2)
    keys = jax.random.split(key, 4)
    first = jax.random.randint(keys[0], (N_REPLICA, 1), 0, N_REPLICA)
    tickets = jnp.arange((N_REPLICA - 1) * MOST) // MOST
    others = (first + 1 + tickets[None, :]) % N_REPLICA
    width = others.shape[1]
    ticket_scores = jax.random.randint(keys[1], others.shape, 0, 1 << 16) * width + jnp.arange(width)[None, :]
    picked = jnp.take_along_axis(others, jnp.argsort(ticket_scores, axis=1)[:, :SEGS - MOST], axis=1)
    owners = jnp.concatenate([jnp.broadcast_to(first, (N_REPLICA, MOST)), picked], axis=1)
    slot_scores = jax.random.randint(keys[2], (N_REPLICA, SEGS), 0, 1 << 16) * SEGS + jnp.arange(SEGS)[None, :]
    owners = jnp.take_along_axis(owners, jnp.argsort(slot_scores, axis=1), axis=1)
    same_owner = owners[:, :, None] == owners[:, None, :]
    earlier = jnp.arange(SEGS)[None, :] < jnp.arange(SEGS)[:, None]
    ranks = jnp.sum(jnp.logical_and(same_owner, earlier[None, :, :]).astype(jnp.int32), axis=2)
    local_scores = jax.random.randint(keys[3], (N_REPLICA, N_REPLICA, ADAPT_DEV), 0, 1 << 16) * ADAPT_DEV + jnp.arange(ADAPT_DEV)
    local_order = jnp.argsort(local_scores, axis=2).astype(jnp.int32)
    local_rows = local_order[jnp.arange(N_REPLICA)[:, None], owners, ranks]
    rows_taken = owners * ADAPT_DEV + local_rows
    return inverse[rows_taken].astype(jnp.int32)


def draw_queries(key, part):
    key = jax.random.fold_in(key, 3)
    values = jnp.clip(jax.random.normal(key, (STEPS, BATCH, QUERY_HEADS * HEAD_SIZE), dtype=jnp.float32), -4.0, 4.0)
    return values.astype(jnp.bfloat16)


def draw_cached_key_rows(key, part):
    key = jax.random.fold_in(key, 4)
    values = jnp.clip(jax.random.normal(key, (BATCH, KV, CACHE, HEAD_SIZE), dtype=jnp.float32), -4.0, 4.0)
    return values.astype(jnp.bfloat16)


def place_ends(result, key, low, high):
    shape = result.shape
    place = [jax.random.randint(jax.random.fold_in(key, axis), (), 0, shape[axis]) for axis in range(len(shape))]
    result = result.at[tuple(place)].set(low)
    longest = shape.index(max(shape))
    place[longest] = (place[longest] + 1) % shape[longest]
    return result.at[tuple(place)].set(high)


def level_of(stream_key, shape, cuts, least, high):
    def one(dim, blocks):
        heights = jax.random.uniform(jax.random.fold_in(jax.random.fold_in(stream_key, 6), dim), (blocks,), jnp.float32, least / len(cuts), high / len(cuts))
        return jnp.repeat(jnp.exp(heights), shape[dim] // blocks).reshape((-1,) + (1,) * (len(shape) - dim - 1))

    loudness = one(*cuts[0])
    for cut in cuts[1:]:
        loudness = loudness * one(*cut)
    return loudness


def split_up(count, total, reach, skew):
    loads = [(1 << 20) // math.isqrt(standing ** skew) + 1 for standing in range(2, count + 1)]
    surplus, given = total - reach - (count - 1), [1] * (count - 1)
    while surplus > 0:
        candidates = [i for i in range(count - 1) if given[i] < reach]
        mass, budget = sum([loads[i] for i in candidates]), surplus
        for i in candidates:
            extra = min(reach - given[i], max(1, budget * loads[i] // mass), surplus)
            given[i] = given[i] + extra
            surplus = surplus - extra
    return np.array([reach] + given)


def ragged(stream_key, amount, total, limit, slope):
    if amount == 2:
        one = jax.random.randint(stream_key, (), max(1, total - limit), min(limit, total - 1) + 1)
        return jnp.stack([one, total - one])
    tallies = jnp.asarray(split_up(amount, total, limit, slope), jnp.int32)
    twos = (amount - 1) // 2
    source_of, taker = tallies[1:1 + 2 * twos:2], tallies[2:2 + 2 * twos:2]
    margin = jnp.minimum(source_of - 1, limit - taker)
    shifted = jax.random.randint(jax.random.fold_in(stream_key, 1), (twos,), 0, 1 << 20) % (margin + 1)
    tallies = tallies.at[1:1 + 2 * twos:2].set(source_of - shifted).at[2:2 + 2 * twos:2].set(taker + shifted)
    return tallies[jax.random.permutation(jax.random.fold_in(stream_key, 2), amount)]


def gaussian(rng, extent, deviation, bound, pieces=(), kind=jnp.bfloat16):
    gain = level_of(rng, extent, pieces, -0.22, 0.18) if pieces else 1.0
    drawn = jax.random.normal(rng, extent, jnp.float32) * deviation * gain
    return jnp.minimum(jnp.maximum(drawn, -bound), bound).astype(kind)


def setup_inputs(seed: int = 0, part: int = 0) -> dict:
    key_of = jax.random.split(jax.random.key(seed), 13)
    own_keys = jax.random.split(jax.random.fold_in(key_of[12], part), 13)
    return {
        "queries": draw_queries(jax.random.fold_in(jax.random.fold_in(key_of[12], part), 71), part),
        "step_keys": gaussian(own_keys[1], (STEPS, BATCH, KV * HEAD_SIZE), 1.0, 4.0, ((1, 8), (2, 2))),
        "step_values": gaussian(own_keys[2], (STEPS, BATCH, KV * HEAD_SIZE), 1.0, 4.0, ((1, 8), (2, 2))),
        "cached_key_rows": draw_cached_key_rows(jax.random.fold_in(jax.random.fold_in(key_of[12], part), 71), part),
        "cached_value_rows": gaussian(own_keys[4], (BATCH, KV, CACHE, HEAD_SIZE), 1.0, 4.0, ((0, 8), (1, 2))),
        "cache_length": place_ends(jax.random.randint(own_keys[5], (BATCH,), 2, CACHE + 1), jax.random.fold_in(own_keys[5], 1), 2, CACHE).astype(jnp.int32),
        "output_weight": gaussian(key_of[6], (QUERY_HEADS * HEAD_SIZE, MODEL_WIDTH), (QUERY_HEADS * HEAD_SIZE) ** -0.5, 0.09375, ((1, 2),)),
        "adapter_down_bank": gaussian(own_keys[7], (ADAPTER_TOTAL, ADAPTER_RANK, QUERY_HEADS * HEAD_SIZE), (QUERY_HEADS * HEAD_SIZE) ** -0.5, 0.09375, ((0, 8), (2, 2))),
        "adapter_up_bank": gaussian(own_keys[8], (ADAPTER_TOTAL, ADAPTER_RANK, MODEL_WIDTH), ADAPTER_RANK ** -0.5, 1.5, ((0, 8), (2, 2))),
        "adapter_bank_row": draw_adapter_bank_row(jax.random.fold_in(jax.random.fold_in(key_of[12], part), 71), part),
        "segment_adapter": draw_segment_adapter(jax.random.fold_in(jax.random.fold_in(key_of[12], part), 71), part),
        "request_segment_index": jax.vmap(lambda own: jnp.searchsorted(jnp.cumsum(ragged(own, SEGS, BATCH_DEV, SEG_MOST, 2)), jnp.arange(BATCH_DEV), side="right"))(jax.random.split(own_keys[11], N_REPLICA)).reshape((N_REPLICA, BATCH_DEV)).astype(jnp.int32),
    }


adapter_scale = 2.0

def attend(queries, step_keys, step_values, cached_key_rows, cached_value_rows, cache_length):
    step_count, batch_rows, width = queries.shape
    kv_count = cached_key_rows.shape[1]
    cache_rows = cached_key_rows.shape[2]
    head_dim = cached_key_rows.shape[3]
    grouped = width // (kv_count * head_dim)
    query_full = queries.astype(jnp.float32).reshape(step_count, batch_rows, kv_count, grouped, head_dim)
    scale_factor = 1.0 / math.sqrt(head_dim)
    cache_scores = jnp.einsum('sbgqd,bgpd->sbgqp', query_full, cached_key_rows.astype(jnp.float32)) * scale_factor
    fresh_keys = step_keys.astype(jnp.float32).reshape(step_count, batch_rows, kv_count, head_dim)
    fresh_scores = jnp.einsum('sbgqd,tbgd->sbgqt', query_full, fresh_keys) * scale_factor
    live_mask = jnp.arange(cache_rows)[None, :] < cache_length[:, None]
    cache_scores = jnp.where(live_mask[None, :, None, None, :], cache_scores, -1e+30)
    causal = jnp.arange(step_count)[None, :] <= jnp.arange(step_count)[:, None]
    fresh_scores = jnp.where(causal[:, None, None, None, :], fresh_scores, -1e+30)
    scores = jnp.concatenate([cache_scores, fresh_scores], axis=-1)
    top_score = lax.optimization_barrier(jnp.max(scores, axis=-1, keepdims=True))
    raised = jnp.exp(scores - top_score)
    weights = (raised / lax.optimization_barrier(jnp.sum(raised, axis=-1, keepdims=True))).astype(jnp.bfloat16)
    cache_part = jnp.einsum('sbgqp,bgpd->sbgqd', weights[..., :cache_rows].astype(jnp.float32), cached_value_rows.astype(jnp.float32))
    fresh_values = step_values.astype(jnp.float32).reshape(step_count, batch_rows, kv_count, head_dim)
    fresh_part = jnp.einsum('sbgqt,tbgd->sbgqd', weights[..., cache_rows:].astype(jnp.float32), fresh_values)
    return (cache_part + fresh_part).reshape(step_count, batch_rows, width).astype(jnp.bfloat16)

def reference(queries, step_keys, step_values, cached_key_rows, cached_value_rows, cache_length, output_weight, adapter_down_bank, adapter_up_bank, adapter_bank_row, segment_adapter, request_segment_index):
    attention_output = attend(queries, step_keys, step_values, cached_key_rows, cached_value_rows, cache_length)
    base_projection = jnp.dot(attention_output.reshape(STEPS * BATCH, QUERY_HEADS * HEAD_SIZE), output_weight, preferred_element_type=jnp.float32)
    base_projection = base_projection.reshape(STEPS, BATCH, MODEL_WIDTH)
    adapters = jnp.take_along_axis(segment_adapter, request_segment_index, axis=1)
    bank_row = adapter_bank_row[adapters].astype(jnp.int32)
    by_group = attention_output.reshape(STEPS, N_REPLICA, BATCH_DEV, QUERY_HEADS * HEAD_SIZE).transpose(1, 0, 2, 3)

    def one_group(packed):
        group_attention, group_batch_rows = packed
        shrink_rows = adapter_down_bank[group_batch_rows].astype(jnp.float32)
        shrunk_features = jnp.einsum('iuf,uof->iuo', group_attention.astype(jnp.float32), shrink_rows).astype(jnp.bfloat16)
        expand_rows = adapter_up_bank[group_batch_rows].astype(jnp.float32)
        return jnp.einsum('fuz,uzy->fuy', shrunk_features.astype(jnp.float32), expand_rows)
    deltas = lax.map(one_group, (by_group, bank_row))
    adapter_delta = deltas.transpose(1, 0, 2, 3).reshape(STEPS, BATCH, MODEL_WIDTH)
    return (base_projection + adapter_scale * adapter_delta).astype(jnp.bfloat16)
```

```python
import math

import jax
import jax.numpy as jnp
from jax import lax
from jax.sharding import PartitionSpec as P

adapter_scale = 2.0


def attend(queries, step_keys, step_values, cached_key_rows, cached_value_rows, cache_length):
    step_count, batch_rows, width = queries.shape
    kv_count = cached_key_rows.shape[1]
    cache_rows = cached_key_rows.shape[2]
    head_dim = cached_key_rows.shape[3]
    grouped = width // (kv_count * head_dim)
    query_full = queries.reshape(step_count, batch_rows, kv_count, grouped, head_dim)
    scale_factor = 1.0 / math.sqrt(head_dim)
    cache_scores = (
        jnp.einsum(
            "sbgqd,bgpd->sbgqp", query_full, cached_key_rows, preferred_element_type=jnp.float32
        )
        * scale_factor
    )
    fresh_keys = step_keys.reshape(step_count, batch_rows, kv_count, head_dim)
    fresh_scores = (
        jnp.einsum("sbgqd,tbgd->sbgqt", query_full, fresh_keys, preferred_element_type=jnp.float32)
        * scale_factor
    )
    live_mask = jnp.arange(cache_rows)[None, :] < cache_length[:, None]
    cache_scores = jnp.where(live_mask[None, :, None, None, :], cache_scores, -1e30)
    causal = jnp.arange(step_count)[None, :] <= jnp.arange(step_count)[:, None]
    fresh_scores = jnp.where(causal[:, None, None, None, :], fresh_scores, -1e30)
    scores = jnp.concatenate([cache_scores, fresh_scores], axis=-1)
    top_score = jnp.max(scores, axis=-1, keepdims=True)
    raised = jnp.exp(scores - top_score)
    weights = (raised / jnp.sum(raised, axis=-1, keepdims=True)).astype(jnp.bfloat16)
    cache_part = jnp.einsum(
        "sbgqp,bgpd->sbgqd",
        weights[..., :cache_rows],
        cached_value_rows,
        preferred_element_type=jnp.float32,
    )
    fresh_values = step_values.reshape(step_count, batch_rows, kv_count, head_dim)
    fresh_part = jnp.einsum(
        "sbgqt,tbgd->sbgqd",
        weights[..., cache_rows:],
        fresh_values,
        preferred_element_type=jnp.float32,
    )
    return (cache_part + fresh_part).reshape(step_count, batch_rows, width).astype(jnp.bfloat16)


def lookup(table, positions):
    entries = table.shape[0]
    hits = positions[:, None] == jnp.arange(entries)[None, :]
    return jnp.sum(jnp.where(hits, table[None, :], 0), axis=1)


def join_heads(rows):
    if lax.axis_size("tensor") != 2:
        return lax.all_gather(rows, "tensor", axis=1, tiled=True)
    other = lax.ppermute(rows, "tensor", [(0, 1), (1, 0)])
    first = lax.axis_index("tensor") == 0
    halves = jnp.where(first, rows, other), jnp.where(first, other, rows)
    return jnp.concatenate(halves, axis=1)


def own_columns(request_bank, bank_size, rank):
    owner_of_column = jnp.arange(bank_size * rank) // rank
    return request_bank[:, None] == owner_of_column[None, :]


def shrink(flat_rows, bank_down, request_bank, step_count):
    bank_size, rank, width = bank_down.shape
    products = jnp.dot(
        flat_rows, bank_down.reshape(bank_size * rank, width).T, preferred_element_type=jnp.float32
    )
    mine = own_columns(request_bank, bank_size, rank)
    products = products.reshape(step_count, -1, bank_size * rank)
    kept = jnp.where(mine[None], products, 0.0)
    kept = kept.reshape(step_count, -1, bank_size * rank // 128, 128)
    folded = jnp.sum(kept, axis=2)
    partial_value = jnp.sum(folded.reshape(step_count, -1, 128 // rank, rank), axis=2)
    return lax.psum(partial_value, "tensor").astype(jnp.bfloat16)


def spread(shrunk, request_bank, bank_size):
    rank = shrunk.shape[-1]
    mine = own_columns(request_bank, bank_size, rank)
    tiled = jnp.tile(shrunk, (1, 1, bank_size))
    doubled = tiled * jnp.bfloat16(adapter_scale)
    return jnp.where(mine[None], doubled, 0).reshape(-1, bank_size * rank)


def shards(
    queries,
    step_keys,
    step_values,
    cached_key_rows,
    cached_value_rows,
    cache_length,
    output_weight,
    adapter_down_bank,
    adapter_up_bank,
    adapter_bank_row,
    segment_adapter,
    request_segment_index,
):
    step_count, batch_rows, width = queries.shape
    attention_output = attend(
        queries, step_keys, step_values, cached_key_rows, cached_value_rows, cache_length
    )
    segment_ids = request_segment_index[0]
    wanted = segment_adapter[0]
    bank_rows = lookup(adapter_bank_row, wanted)
    bank_down = lax.all_gather(adapter_down_bank, "replica", axis=0, tiled=True)
    bank_up = lax.all_gather(adapter_up_bank, "replica", axis=0, tiled=True)
    request_bank = lookup(bank_rows, segment_ids)
    bank_size, rank, columns = bank_up.shape
    flat_rows = attention_output.reshape(step_count * batch_rows, width)
    shrunk = shrink(flat_rows, bank_down, request_bank, step_count)
    base_projection = jnp.dot(
        join_heads(flat_rows),
        output_weight,
        preferred_element_type=jnp.float32,
    )
    own_shrunk = spread(shrunk, request_bank, bank_size)
    base_projection, own_shrunk = lax.optimization_barrier((base_projection, own_shrunk))
    adapter_delta = jnp.dot(
        own_shrunk,
        bank_up.reshape(bank_size * rank, columns),
        preferred_element_type=jnp.float32,
    )
    projected = (base_projection + adapter_delta).astype(jnp.bfloat16)
    return projected.reshape(step_count, batch_rows, columns)


def solution(mesh):
    return jax.shard_map(
        shards,
        mesh=mesh,
        in_specs=(
            P(None, ("parts", "replica"), "tensor"),
            P(None, ("parts", "replica"), "tensor"),
            P(None, ("parts", "replica"), "tensor"),
            P(("parts", "replica"), "tensor", None, None),
            P(("parts", "replica"), "tensor", None, None),
            P(("parts", "replica")),
            P(None, "tensor"),
            P(("parts", "replica"), None, "tensor"),
            P(("parts", "replica"), None, "tensor"),
            P("parts"),
            P(("parts", "replica"), None),
            P(("parts", "replica"), None),
        ),
        out_specs=P(None, ("parts", "replica"), "tensor"),
        check_vma=False,
    )
```

```python
import math

import jax
import jax.numpy as jnp
from jax import lax
from jax.sharding import PartitionSpec as P

adapter_scale = 2.0


def attend(queries, step_keys, step_values, cached_key_rows, cached_value_rows, cache_length):
    step_count, batch_rows, width = queries.shape
    kv_count = cached_key_rows.shape[1]
    cache_rows = cached_key_rows.shape[2]
    head_dim = cached_key_rows.shape[3]
    grouped = width // (kv_count * head_dim)
    query_full = queries.reshape(step_count, batch_rows, kv_count, grouped, head_dim)
    scale_factor = 1.0 / math.sqrt(head_dim)
    cache_scores = (
        jnp.einsum(
            "sbgqd,bgpd->sbgqp", query_full, cached_key_rows, preferred_element_type=jnp.float32
        )
        * scale_factor
    )
    fresh_keys = step_keys.reshape(step_count, batch_rows, kv_count, head_dim)
    fresh_scores = (
        jnp.einsum("sbgqd,tbgd->sbgqt", query_full, fresh_keys, preferred_element_type=jnp.float32)
        * scale_factor
    )
    live_mask = jnp.arange(cache_rows)[None, :] < cache_length[:, None]
    cache_scores = jnp.where(live_mask[None, :, None, None, :], cache_scores, -1e30)
    causal = jnp.arange(step_count)[None, :] <= jnp.arange(step_count)[:, None]
    fresh_scores = jnp.where(causal[:, None, None, None, :], fresh_scores, -1e30)
    scores = jnp.concatenate([cache_scores, fresh_scores], axis=-1)
    top_score = jnp.max(scores, axis=-1, keepdims=True)
    raised = jnp.exp(scores - top_score)
    weights = (raised / jnp.sum(raised, axis=-1, keepdims=True)).astype(jnp.bfloat16)
    cache_part = jnp.einsum(
        "sbgqp,bgpd->sbgqd",
        weights[..., :cache_rows],
        cached_value_rows,
        preferred_element_type=jnp.float32,
    )
    fresh_values = step_values.reshape(step_count, batch_rows, kv_count, head_dim)
    fresh_part = jnp.einsum(
        "sbgqt,tbgd->sbgqd",
        weights[..., cache_rows:],
        fresh_values,
        preferred_element_type=jnp.float32,
    )
    return (cache_part + fresh_part).reshape(step_count, batch_rows, width).astype(jnp.bfloat16)


def lookup(table, positions):
    entries = table.shape[0]
    hits = positions[:, None] == jnp.arange(entries)[None, :]
    return jnp.sum(jnp.where(hits, table[None, :], 0), axis=1)


def join_heads(rows):
    if lax.axis_size("tensor") != 2:
        return lax.all_gather(rows, "tensor", axis=1, tiled=True)
    other = lax.ppermute(rows, "tensor", [(0, 1), (1, 0)])
    first = lax.axis_index("tensor") == 0
    halves = jnp.where(first, rows, other), jnp.where(first, other, rows)
    return jnp.concatenate(halves, axis=1)


def own_columns(request_bank, blocks, block_size, rank):
    columns = jnp.arange(block_size * rank)
    owner_of_column = jnp.concatenate([block * block_size + columns // rank for block in blocks])
    return request_bank[:, None] == owner_of_column[None, :]


def shrink(flat_rows, bank_down, request_bank, step_count):
    bank_size, rank, width = bank_down.shape
    products = jnp.dot(
        flat_rows, bank_down.reshape(bank_size * rank, width).T, preferred_element_type=jnp.float32
    )
    mine = own_columns(request_bank, [0], bank_size, rank)
    products = products.reshape(step_count, -1, bank_size * rank)
    kept = jnp.where(mine[None], products, 0.0)
    kept = kept.reshape(step_count, -1, bank_size * rank // 128, 128)
    folded = jnp.sum(kept, axis=2)
    partial_value = jnp.sum(folded.reshape(step_count, -1, 128 // rank, rank), axis=2)
    return lax.psum(partial_value, "tensor").astype(jnp.bfloat16)


def spread(shrunk, mine):
    rank = shrunk.shape[-1]
    width = mine.shape[1]
    tiled = jnp.tile(shrunk, (1, 1, width // rank))
    doubled = tiled * jnp.bfloat16(adapter_scale)
    return jnp.where(mine[None], doubled, 0).reshape(-1, width)


def pairs(*hops):
    return [(2 * here + core, 2 * there + core) for here, there in hops for core in (0, 1)]


def relayed_delta(joined, weight, shrunk, request_bank, up_bank, cuts):
    block_size, rank, columns = up_bank.shape
    inward, across, outward = pairs((0, 1), (3, 2)), pairs((1, 2), (2, 1)), pairs((1, 0), (2, 3))
    swap = [(2 * place + core, 2 * place + 1 - core) for place in range(4) for core in (0, 1)]
    index = lax.axis_index("replica")
    place, core = index // 2, index % 2
    inner = (place == 1) | (place == 2)
    edge = jnp.where(place < 2, 0, 3)
    places = [place, 3 - place, edge, 3 - edge]
    blocks = [2 * p + core for p in places] + [2 * p + 1 - core for p in places]
    chunks = [up_bank[:, :, a:b].reshape(block_size * rank, b - a) for a, b in cuts]
    outer_chunks = [lax.ppermute(chunk, "replica", inward) for chunk in chunks]
    held = []
    for chunk, outer in zip(chunks, outer_chunks):
        facing = lax.ppermute(chunk, "replica", across)
        far = lax.ppermute(outer, "replica", across)
        mine = jnp.concatenate([chunk, facing, outer, far], axis=0)
        held.append((mine, lax.ppermute(mine, "replica", swap)))
    outer_bank = lax.ppermute(request_bank, "replica", inward)
    outer_shrunk = lax.ppermute(shrunk, "replica", inward)
    outer_left = spread(outer_shrunk, own_columns(outer_bank, blocks, block_size, rank))
    half = outer_left.shape[1] // 2

    def product(left, bank):
        return jnp.dot(
            left[:, :half], bank[0], preferred_element_type=jnp.float32
        ) + jnp.dot(left[:, half:], bank[1], preferred_element_type=jnp.float32)

    for_outer = [product(outer_left, bank).astype(jnp.bfloat16) for bank in held]
    for_outer[-1], joined, shrunk = lax.optimization_barrier((for_outer[-1], joined, shrunk))
    returned = [lax.ppermute(part, "replica", outward) for part in for_outer]
    base = jnp.dot(joined, weight, preferred_element_type=jnp.float32)
    own_left = spread(shrunk, own_columns(request_bank, blocks, block_size, rank))
    own = [product(own_left, bank) for bank in held]
    base, own[-1], returned[-1] = lax.optimization_barrier((base, own[-1], returned[-1]))
    deltas = [
        jnp.where(inner, mine, back.astype(jnp.float32)) for mine, back in zip(own, returned)
    ]
    return base, shrunk, deltas


def shards(
    queries,
    step_keys,
    step_values,
    cached_key_rows,
    cached_value_rows,
    cache_length,
    output_weight,
    adapter_down_bank,
    adapter_up_bank,
    adapter_bank_row,
    segment_adapter,
    request_segment_index,
):
    step_count, batch_rows, width = queries.shape
    attention_output = attend(
        queries, step_keys, step_values, cached_key_rows, cached_value_rows, cache_length
    )
    segment_ids = request_segment_index[0]
    wanted = segment_adapter[0]
    bank_rows = lookup(adapter_bank_row, wanted)
    bank_down = lax.all_gather(adapter_down_bank, "replica", axis=0, tiled=True)
    block_size, rank, columns = adapter_up_bank.shape
    relay = lax.axis_size("replica") == 8 and columns % 512 == 0
    direct = columns // 4 if relay else columns
    bank_up = lax.all_gather(adapter_up_bank[:, :, :direct], "replica", axis=0, tiled=True)
    bank_size = bank_up.shape[0]
    request_bank = lookup(bank_rows, segment_ids)
    flat_rows = attention_output.reshape(step_count * batch_rows, width)
    shrunk = shrink(flat_rows, bank_down, request_bank, step_count)
    joined, shrunk = lax.optimization_barrier((join_heads(flat_rows), shrunk))
    relayed = []
    if relay:
        cuts = [(k * direct, (k + 1) * direct) for k in range(1, 4)]
        base_projection, shrunk, relayed = relayed_delta(
            joined, output_weight, shrunk, request_bank, adapter_up_bank, cuts
        )
    else:
        base_projection = jnp.dot(joined, output_weight, preferred_element_type=jnp.float32)
    own_shrunk = spread(shrunk, own_columns(request_bank, [0], bank_size, rank))
    direct_delta = jnp.dot(
        own_shrunk,
        bank_up.reshape(bank_size * rank, direct),
        preferred_element_type=jnp.float32,
    )
    deltas = [direct_delta] + relayed
    projected = (base_projection + jnp.concatenate(deltas, axis=1)).astype(jnp.bfloat16)
    return projected.reshape(step_count, batch_rows, columns)


def solution(mesh):
    return jax.shard_map(
        shards,
        mesh=mesh,
        in_specs=(
            P(None, ("parts", "replica"), "tensor"),
            P(None, ("parts", "replica"), "tensor"),
            P(None, ("parts", "replica"), "tensor"),
            P(("parts", "replica"), "tensor", None, None),
            P(("parts", "replica"), "tensor", None, None),
            P(("parts", "replica")),
            P(None, "tensor"),
            P(("parts", "replica"), None, "tensor"),
            P(("parts", "replica"), None, "tensor"),
            P("parts"),
            P(("parts", "replica"), None),
            P(("parts", "replica"), None),
        ),
        out_specs=P(None, ("parts", "replica"), "tensor"),
        check_vma=False,
    )
```

```python
import math

import jax
import jax.numpy as jnp
from jax import lax
from jax.sharding import PartitionSpec as P

adapter_scale = 2.0


def attend(
    queries, step_keys, step_values, cached_key_rows, cached_value_rows, cache_length, beside
):
    step_count, batch_rows, width = queries.shape
    kv_count = cached_key_rows.shape[1]
    cache_rows = cached_key_rows.shape[2]
    head_dim = cached_key_rows.shape[3]
    grouped = width // (kv_count * head_dim)
    query_full = queries.reshape(step_count, batch_rows, kv_count, grouped, head_dim)
    scale_factor = 1.0 / math.sqrt(head_dim)
    cache_scores = (
        jnp.einsum(
            "sbgqd,bgpd->sbgqp", query_full, cached_key_rows, preferred_element_type=jnp.float32
        )
        * scale_factor
    )
    fresh_keys = step_keys.reshape(step_count, batch_rows, kv_count, head_dim)
    fresh_scores = (
        jnp.einsum("sbgqd,tbgd->sbgqt", query_full, fresh_keys, preferred_element_type=jnp.float32)
        * scale_factor
    )
    cache_scores, beside = lax.optimization_barrier((cache_scores, beside))
    live_mask = jnp.arange(cache_rows)[None, :] < cache_length[:, None]
    cache_scores = jnp.where(live_mask[None, :, None, None, :], cache_scores, -1e30)
    causal = jnp.arange(step_count)[None, :] <= jnp.arange(step_count)[:, None]
    fresh_scores = jnp.where(causal[:, None, None, None, :], fresh_scores, -1e30)
    scores = jnp.concatenate([cache_scores, fresh_scores], axis=-1)
    top_score = jnp.max(scores, axis=-1, keepdims=True)
    raised = jnp.exp(scores - top_score)
    weights = (raised / jnp.sum(raised, axis=-1, keepdims=True)).astype(jnp.bfloat16)
    cache_part = jnp.einsum(
        "sbgqp,bgpd->sbgqd",
        weights[..., :cache_rows],
        cached_value_rows,
        preferred_element_type=jnp.float32,
    )
    fresh_values = step_values.reshape(step_count, batch_rows, kv_count, head_dim)
    fresh_part = jnp.einsum(
        "sbgqt,tbgd->sbgqd",
        weights[..., cache_rows:],
        fresh_values,
        preferred_element_type=jnp.float32,
    )
    attended = (cache_part + fresh_part).reshape(step_count, batch_rows, width)
    return attended.astype(jnp.bfloat16), beside


def lookup(table, positions):
    entries = table.shape[0]
    hits = positions[:, None] == jnp.arange(entries)[None, :]
    return jnp.sum(jnp.where(hits, table[None, :], 0), axis=1)


def swap_heads(rows):
    if lax.axis_size("tensor") != 2:
        return lax.all_gather(rows, "tensor", axis=1, tiled=True)
    return lax.ppermute(rows, "tensor", [(0, 1), (1, 0)])


def join_heads(rows, other):
    if lax.axis_size("tensor") != 2:
        return other
    first = lax.axis_index("tensor") == 0
    halves = jnp.where(first, rows, other), jnp.where(first, other, rows)
    return jnp.concatenate(halves, axis=1)


def own_columns(request_bank, blocks, block_size, rank):
    columns = jnp.arange(block_size * rank)
    owner_of_column = jnp.concatenate([block * block_size + columns // rank for block in blocks])
    return request_bank[:, None] == owner_of_column[None, :]


def shrink(flat_rows, bank_down, request_bank, step_count):
    bank_size, rank, width = bank_down.shape
    products = jnp.dot(
        flat_rows, bank_down.reshape(bank_size * rank, width).T, preferred_element_type=jnp.float32
    )
    mine = own_columns(request_bank, [0], bank_size, rank)
    products = products.reshape(step_count, -1, bank_size * rank)
    kept = jnp.where(mine[None], products, 0.0)
    kept = kept.reshape(step_count, -1, bank_size * rank // 128, 128)
    folded = jnp.sum(kept, axis=2)
    partial_value = jnp.sum(folded.reshape(step_count, -1, 128 // rank, rank), axis=2)
    return lax.psum(partial_value, "tensor").astype(jnp.bfloat16)


def spread(shrunk, mine):
    rank = shrunk.shape[-1]
    width = mine.shape[1]
    tiled = jnp.tile(shrunk, (1, 1, width // rank))
    doubled = tiled * jnp.bfloat16(adapter_scale)
    return jnp.where(mine[None], doubled, 0).reshape(-1, width)


def pairs(*hops):
    return [(2 * here + core, 2 * there + core) for here, there in hops for core in (0, 1)]


def first_hop(chunks):
    inward, across = pairs((0, 1), (3, 2)), pairs((1, 2), (2, 1))
    outer = [lax.ppermute(chunk, "replica", inward) for chunk in chunks]
    facing = [lax.ppermute(chunk, "replica", across) for chunk in chunks]
    return chunks, outer, facing


def second_hop(hop):
    far = [lax.ppermute(chunk, "replica", pairs((1, 2), (2, 1))) for chunk in hop[1]]
    return hop + (far,)


def relayed_delta(halves, weight, shrunk, request_bank, hops, block_size, rank):
    inward, outward = pairs((0, 1), (3, 2)), pairs((1, 0), (2, 3))
    swap = [(2 * place + core, 2 * place + 1 - core) for place in range(4) for core in (0, 1)]
    index = lax.axis_index("replica")
    place, core = index // 2, index % 2
    inner = (place == 1) | (place == 2)
    edge = jnp.where(place < 2, 0, 3)
    places = [place, 3 - place, edge, 3 - edge]
    blocks = [2 * p + core for p in places] + [2 * p + 1 - core for p in places]
    held = []
    for chunk, outer, facing, far in zip(*hops):
        mine = jnp.concatenate([chunk, facing, outer, far], axis=0)
        held.append((mine, lax.ppermute(mine, "replica", swap)))
    outer_bank = lax.ppermute(request_bank, "replica", inward)
    outer_shrunk = lax.ppermute(shrunk, "replica", inward)
    outer_left = spread(outer_shrunk, own_columns(outer_bank, blocks, block_size, rank))
    half = outer_left.shape[1] // 2

    def product(left, bank):
        return jnp.dot(
            left[:, :half], bank[0], preferred_element_type=jnp.float32
        ) + jnp.dot(left[:, half:], bank[1], preferred_element_type=jnp.float32)

    for_outer = [product(outer_left, bank).astype(jnp.bfloat16) for bank in held]
    for_outer[-1], halves, shrunk = lax.optimization_barrier((for_outer[-1], halves, shrunk))
    returned = [lax.ppermute(part, "replica", outward) for part in for_outer]
    base = jnp.dot(join_heads(*halves), weight, preferred_element_type=jnp.float32)
    own_left = spread(shrunk, own_columns(request_bank, blocks, block_size, rank))
    own = [product(own_left, bank) for bank in held]
    base, own[-1], returned[-1] = lax.optimization_barrier((base, own[-1], returned[-1]))
    deltas = [
        jnp.where(inner, mine, back.astype(jnp.float32)) for mine, back in zip(own, returned)
    ]
    return base, shrunk, deltas


def shards(
    queries,
    step_keys,
    step_values,
    cached_key_rows,
    cached_value_rows,
    cache_length,
    output_weight,
    adapter_down_bank,
    adapter_up_bank,
    adapter_bank_row,
    segment_adapter,
    request_segment_index,
):
    step_count, batch_rows, width = queries.shape
    block_size, rank, columns = adapter_up_bank.shape
    relay = lax.axis_size("replica") == 8 and columns % 512 == 0
    direct = columns // 4 if relay else columns
    hops = ()
    if relay:
        rest = [adapter_up_bank[:, :, k * direct : (k + 1) * direct] for k in range(1, 4)]
        hops = first_hop([chunk.reshape(block_size * rank, direct) for chunk in rest])
    attention_output, hops = attend(
        queries, step_keys, step_values, cached_key_rows, cached_value_rows, cache_length, hops
    )
    segment_ids = request_segment_index[0]
    wanted = segment_adapter[0]
    bank_rows = lookup(adapter_bank_row, wanted)
    bank_down = lax.all_gather(adapter_down_bank, "replica", axis=0, tiled=True)
    bank_up = lax.all_gather(adapter_up_bank[:, :, :direct], "replica", axis=0, tiled=True)
    bank_size = bank_up.shape[0]
    request_bank = lookup(bank_rows, segment_ids)
    flat_rows = attention_output.reshape(step_count * batch_rows, width)
    if relay:
        hops = second_hop(hops)
        bank_down, hops = lax.optimization_barrier((bank_down, hops))
    shrunk = shrink(flat_rows, bank_down, request_bank, step_count)
    halves = (flat_rows, swap_heads(flat_rows))
    relayed = []
    if relay:
        base_projection, shrunk, relayed = relayed_delta(
            halves, output_weight, shrunk, request_bank, hops, block_size, rank
        )
    else:
        base_projection = jnp.dot(
            join_heads(*halves), output_weight, preferred_element_type=jnp.float32
        )
    base_projection, shrunk = lax.optimization_barrier((base_projection, shrunk))
    own_shrunk = spread(shrunk, own_columns(request_bank, [0], bank_size, rank))
    direct_delta = jnp.dot(
        own_shrunk,
        bank_up.reshape(bank_size * rank, direct),
        preferred_element_type=jnp.float32,
    )
    deltas = [direct_delta] + relayed
    projected = (base_projection + jnp.concatenate(deltas, axis=1)).astype(jnp.bfloat16)
    return projected.reshape(step_count, batch_rows, columns)


def solution(mesh):
    return jax.shard_map(
        shards,
        mesh=mesh,
        in_specs=(
            P(None, ("parts", "replica"), "tensor"),
            P(None, ("parts", "replica"), "tensor"),
            P(None, ("parts", "replica"), "tensor"),
            P(("parts", "replica"), "tensor", None, None),
            P(("parts", "replica"), "tensor", None, None),
            P(("parts", "replica")),
            P(None, "tensor"),
            P(("parts", "replica"), None, "tensor"),
            P(("parts", "replica"), None, "tensor"),
            P("parts"),
            P(("parts", "replica"), None),
            P(("parts", "replica"), None),
        ),
        out_specs=P(None, ("parts", "replica"), "tensor"),
        check_vma=False,
    )
```
